32 devices in a mesh: rve: 2 (over x), branch: 16 (over z, y, core).
Axes of the slice: x: 2, y: 2, z: 4, core: 2. Of those that a mesh axis runs over, the one named last changes fastest.
Arguments:
- loads: bfloat16 [2048, 32, 192], P(('rve', 'branch')), parts along dimension 0, may hold values from -6 to 6
- basis: bfloat16 [2048, 32, 192], P(('rve', 'branch')), parts along dimension 0, may hold values from -0.4375 to 0.4375
- transfer: bfloat16 [2048, 32, 32], P(('rve', 'branch')), parts along dimension 0, may hold values from -0.375 to 0.375
- near_blocks: bfloat16 [3072, 192, 192], P(('rve', 'branch')), parts along dimension 0, may hold values from -0.4375 to 0.4375
- near_src: int32 [3072], P(('rve', 'branch')), parts along dimension 0, may hold values from -1 to 1023, as said below
- near_tgt: int32 [3072], P(('rve', 'branch')), parts along dimension 0, may hold values from 0 to 1023, as said below
- far_blocks: bfloat16 [8192, 32, 32], P(('rve', 'branch')), parts along dimension 0, may hold values from -1 to 1
- far_src: int32 [8192], P(('rve', 'branch')), parts along dimension 0, may hold values from -1 to 1023, as said below
- far_tgt: int32 [8192], P(('rve', 'branch')), parts along dimension 0, may hold values from 0 to 1023, as said below
- coarse_blocks: bfloat16 [2048, 32, 32], P(('rve', 'branch')), parts along dimension 0, may hold values from -1 to 1
- coarse_src: int32 [2048], P(('rve', 'branch')), parts along dimension 0, may hold values from -1 to 127, as said below
- coarse_tgt: int32 [2048], P(('rve', 'branch')), parts along dimension 0, may hold values from 0 to 127, as said below
Outputs:
- response: bfloat16 [2048, 32, 192], P(('rve', 'branch')), parts along dimension 0
The draws below stay inside these ranges and needn't reach their ends.
There are 2 independent parts, one for each index of `rve`. The reference program is written for one: setup_inputs(seed, part) draws one part's arguments, and reference() takes and returns one part's arrays. A program takes and returns all parts, laid end to end along the dimension named above; each array names one. Nothing has to cross between parts.
Inputs may be any that keep to these rules, and one draw needn't show every extreme that they name: `near_src`: entries of one device's block of 96 name -1 or a leaf at most 64 leaves before the device's first leaf or after its last one. `near_tgt`: entries of one device's block of 96 name leaves of that device. `far_src`: in one device's block of 256 entries at most 32 name leaves of any one device, and exactly 32 name leaves of some device; at least half of the entries are not -1. `far_tgt`: entries of one device's block of 256 name leaves of that device. `coarse_src`: in one device's block of 64 entries at most 8 name parents held by any one device (parents q with q // 8 equal), and exactly 8 for some device; at least half are not -1. `coarse_tgt`: entries of one device's block of 64 name parents of that device's leaves.
All inputs are finite; a program needn't handle non-finite values.
Results may differ from the reference program's by a relative error of at most 0.005.
Values may be sent and summed in bfloat16 or wider, within the bound.
A program may use at most 128 MiB of HBM per device.

```python
import jax
import jax.numpy as jnp
from jax import lax

RANK = 32
CASES = 32
LEAF_DEV = 64
P3 = 192
PAR_DEV = 8
NEAR_DEV = 96
FAR_DEV = 256
COARSE_DEV = 64
NLEAF = 1024
N_BRANCH = 16


def pick_sources(key_base, devices, per_device, count):
    capacity = 2 * count // devices
    slots = devices * capacity

    def one_device(device):
        key_device = jax.random.fold_in(key_base, device)
        key_perm, key_star, key_leaf, key_live = jax.random.split(key_device, 4)
        shuffled = jax.random.permutation(key_perm, slots)
        position = jnp.argsort(shuffled).astype(jnp.int32)
        star = jax.random.randint(key_star, (), 0, devices)
        owners_all = jnp.arange(slots, dtype=jnp.int32) // capacity
        score = position + jnp.where(owners_all == star, -slots, 0).astype(jnp.int32)
        chosen = jnp.argsort(score)[:count].astype(jnp.int32)
        owner = chosen // capacity
        within = jax.random.randint(key_leaf, (count,), 0, per_device)
        live = jax.random.randint(key_live, (), count // 2, count + 1)
        return jnp.where(jnp.arange(count) < live, owner * per_device + within, -1).astype(jnp.int32)
    return jax.vmap(one_device)(jnp.arange(devices)).reshape(-1)


def local_targets(key_base, devices, per_device, count):
    within = jax.random.randint(key_base, (devices, count), 0, per_device)
    return (within + jnp.arange(devices, dtype=jnp.int32)[:, None] * per_device).reshape(-1).astype(jnp.int32)


def draw_near_src(key, part):
    key = jax.random.fold_in(key, 3)
    key_offset, key_empty = jax.random.split(key)
    devices = NLEAF // LEAF_DEV
    offset = jax.random.randint(key_offset, (devices, NEAR_DEV), -LEAF_DEV, 2 * LEAF_DEV)
    source = jnp.arange(devices, dtype=jnp.int32)[:, None] * LEAF_DEV + offset
    keep = jax.random.randint(key_empty, (devices, NEAR_DEV), 0, 8) > 0
    inside = (source >= 0) & (source < NLEAF) & keep
    return jnp.where(inside, source, -1).reshape(-1).astype(jnp.int32)


def draw_near_tgt(key, part):
    key = jax.random.fold_in(key, 5)
    return local_targets(key, NLEAF // LEAF_DEV, LEAF_DEV, NEAR_DEV)


def draw_far_src(key, part):
    key = jax.random.fold_in(key, 7)
    return pick_sources(key, NLEAF // LEAF_DEV, LEAF_DEV, FAR_DEV)


def draw_far_tgt(key, part):
    key = jax.random.fold_in(key, 11)
    return local_targets(key, NLEAF // LEAF_DEV, LEAF_DEV, FAR_DEV)


def draw_coarse_src(key, part):
    key = jax.random.fold_in(key, 13)
    return pick_sources(key, NLEAF // LEAF_DEV, PAR_DEV, COARSE_DEV)


def draw_coarse_tgt(key, part):
    key = jax.random.fold_in(key, 17)
    return local_targets(key, NLEAF // LEAF_DEV, PAR_DEV, COARSE_DEV)


def levels(stream_key, extent, cuts, smallest, top_value):
    level = 1.0
    for dim, blocks in cuts:
        draws = jax.random.uniform(jax.random.fold_in(jax.random.fold_in(stream_key, 6), dim), (blocks,), jnp.float32, smallest / len(cuts), top_value / len(cuts))
        level = level * jnp.repeat(jnp.exp(draws), extent[dim] // blocks).reshape((-1,) + (1,) * (len(extent) - 1 - dim))
    return level


def scatter_about(own_key, extent, deviation, reach, cuts=(), held_as=jnp.bfloat16):
    values = jax.random.normal(own_key, extent, jnp.float32) * deviation
    if len(cuts) > 0:
        values = levels(own_key, extent, cuts, -0.22, 0.18) * values
    return jnp.clip(values, min=-reach, max=reach).astype(held_as)


def setup_inputs(seed: int = 0, part: int = 0) -> dict:
    key_of = jax.random.split(jax.random.key(seed), 13)
    part_keys = jax.random.split(jax.random.fold_in(key_of[12], part), 13)
    loads = scatter_about(part_keys[0], (NLEAF, CASES, P3), 1.0, 6.0, ((0, 16),))
    basis = scatter_about(part_keys[1], (NLEAF, RANK, P3), P3 ** -0.5, 0.4375, ((0, 16),))
    transfer = scatter_about(part_keys[2], (NLEAF, RANK, RANK), (8 * RANK) ** -0.5, 0.375, ((0, 16),))
    near_blocks = scatter_about(part_keys[3], (N_BRANCH * NEAR_DEV, P3, P3), P3 ** -0.5, 0.4375, ((0, 16),))
    near_src = draw_near_src(jax.random.fold_in(jax.random.fold_in(key_of[12], part), 71), part)
    near_tgt = draw_near_tgt(jax.random.fold_in(jax.random.fold_in(key_of[12], part), 71), part)
    far_blocks = scatter_about(part_keys[6], (N_BRANCH * FAR_DEV, RANK, RANK), RANK ** -0.5, 1.0, ((0, 16),))
    far_src = draw_far_src(jax.random.fold_in(jax.random.fold_in(key_of[12], part), 71), part)
    far_tgt = draw_far_tgt(jax.random.fold_in(jax.random.fold_in(key_of[12], part), 71), part)
    coarse_blocks = scatter_about(part_keys[9], (N_BRANCH * COARSE_DEV, RANK, RANK), RANK ** -0.5, 1.0, ((0, 16),))
    coarse_src = draw_coarse_src(jax.random.fold_in(jax.random.fold_in(key_of[12], part), 71), part)
    coarse_tgt = draw_coarse_tgt(jax.random.fold_in(jax.random.fold_in(key_of[12], part), 71), part)
    return dict(loads=loads, basis=basis, transfer=transfer, near_blocks=near_blocks, near_src=near_src, near_tgt=near_tgt, far_blocks=far_blocks, far_src=far_src, far_tgt=far_tgt, coarse_blocks=coarse_blocks, coarse_src=coarse_src, coarse_tgt=coarse_tgt)


def reference(loads, basis, transfer, near_blocks, near_src, near_tgt, far_blocks, far_src, far_tgt, coarse_blocks, coarse_src, coarse_tgt):
    nleaf, cases, width = loads.shape
    rank = basis.shape[1]
    nparent = nleaf // 8
    leaf_coef = jnp.einsum("lcp,lrp->lcr", loads.astype(jnp.float32), basis.astype(jnp.float32)).astype(jnp.bfloat16)
    lifted = jnp.einsum("lcr,lrs->lcs", leaf_coef.astype(jnp.float32), transfer.astype(jnp.float32))
    parent_coef = lifted.reshape(nparent, 8, cases, rank).sum(axis=1).astype(jnp.bfloat16)
    far_live = (far_src >= 0).astype(jnp.float32)
    far_rows = jnp.take(leaf_coef, jnp.clip(far_src, 0, nleaf - 1).astype(jnp.int32), axis=0).astype(jnp.float32)
    far_terms = jnp.einsum("ncr,nrs->ncs", far_rows, far_blocks.astype(jnp.float32)) * far_live[:, None, None]
    far_field = jax.ops.segment_sum(far_terms, far_tgt, num_segments=nleaf)
    coarse_live = (coarse_src >= 0).astype(jnp.float32)
    coarse_rows = jnp.take(parent_coef, jnp.clip(coarse_src, 0, nparent - 1).astype(jnp.int32), axis=0).astype(jnp.float32)
    coarse_terms = jnp.einsum("ncr,nrs->ncs", coarse_rows, coarse_blocks.astype(jnp.float32)) * coarse_live[:, None, None]
    coarse_field = jax.ops.segment_sum(coarse_terms, coarse_tgt, num_segments=nparent).astype(jnp.bfloat16)
    downward = jnp.einsum("lcs,lrs->lcr", jnp.repeat(coarse_field, 8, axis=0).astype(jnp.float32), transfer.astype(jnp.float32))
    local_coef = (far_field + downward).astype(jnp.bfloat16)
    far_out = jnp.einsum("lcr,lrp->lcp", local_coef.astype(jnp.float32), basis.astype(jnp.float32))
    groups = N_BRANCH
    blocks_grouped = near_blocks.reshape(groups, -1, width, width)
    sources_grouped = near_src.reshape(groups, -1)
    targets_grouped = near_tgt.reshape(groups, -1)

    def add_group(total, pieces):
        blocks, sources, targets = pieces
        live = (sources >= 0).astype(jnp.float32)
        picked = jnp.take(loads, jnp.clip(sources, 0, nleaf - 1).astype(jnp.int32), axis=0).astype(jnp.float32)
        terms = jnp.einsum("ncp,npq->ncq", picked, blocks.astype(jnp.float32)) * live[:, None, None]
        return total.at[targets].add(terms), None

    near_field, _ = lax.scan(add_group, jnp.zeros((nleaf, cases, width), jnp.float32), (blocks_grouped, sources_grouped, targets_grouped))
    return (far_out + near_field).astype(jnp.bfloat16)
```

```python
import jax
import jax.numpy as jnp
from jax import lax
from jax.experimental import pallas as pl
from jax.experimental.pallas import tpu as pltpu
from jax.sharding import PartitionSpec as P

F32, BF16 = jnp.float32, jnp.bfloat16
VMEM = pl.BlockSpec(memory_space=pltpu.VMEM)
SMEM = pl.BlockSpec(memory_space=pltpu.SMEM)
PACK = 4
NT = (((1,), (1,)), ((), ()))


def div(x, n):
    return lax.shift_right_logical(x, n.bit_length() - 1) if n & (n - 1) == 0 else lax.div(x, n)


def dot(a, b):
    return jnp.dot(a, b, preferred_element_type=F32)


def dot_nt(a, b):
    return lax.dot_general(a, b, NT, preferred_element_type=F32)


def lane_slot(shape, rank):
    return div(lax.broadcasted_iota(jnp.int32, shape, 1), rank)


def upward(loads_ref, basis_ref, transfer_ref, out_ref):
    leaves, cases, width = loads_ref.shape
    rank = basis_ref.shape[1]
    groups = leaves // PACK
    slot = lane_slot((cases, PACK * rank), rank)
    per_parent = 8 // PACK
    parents = []
    total = None
    for g in range(groups):
        part = pl.ds(PACK * g, PACK)
        full = dot_nt(
            loads_ref[part].reshape(PACK * cases, width), basis_ref[part].reshape(PACK * rank, width)
        )
        packed = full[:cases]
        for k in range(1, PACK):
            packed = jnp.where(slot == k, full[k * cases : (k + 1) * cases], packed)
        packed = packed.astype(BF16)
        out_ref[g] = packed
        term = dot(packed, transfer_ref[part].reshape(PACK * rank, rank))
        total = term if g % per_parent == 0 else total + term
        if g % per_parent == per_parent - 1:
            parents.append(total)
    for h in range(len(parents) // PACK):
        out_ref[groups + h] = jnp.concatenate(parents[PACK * h : PACK * h + PACK], axis=1).astype(BF16)


def near(src_ref, tgt_ref, left_ref, own_ref, right_ref, blocks_ref, out_ref, wide):
    step = pl.program_id(0)
    leaves = own_ref.shape[0]
    base = lax.axis_index("branch") * leaves
    chunk = blocks_ref.shape[0]

    @pl.when(step == 0)
    def _():
        wide[pl.ds(0, leaves)] = left_ref[...]
        wide[pl.ds(leaves, leaves)] = own_ref[...]
        wide[pl.ds(2 * leaves, leaves)] = right_ref[...]
        wide[3 * leaves] = jnp.zeros(wide.shape[1:], BF16)
        out_ref[...] = jnp.zeros_like(out_ref)

    terms = []
    for i in range(chunk):
        s = src_ref[step * chunk + i]
        row = jnp.where(s < 0, 3 * leaves, jnp.clip(s - base + leaves, 0, 3 * leaves - 1))
        terms.append(dot(wide[row], blocks_ref[i]))
    for i in range(chunk):
        t = jnp.clip(tgt_ref[step * chunk + i] - base, 0, leaves - 1)
        out_ref[t] += terms[i]


def downward(
    fsrc_ref, ftgt_ref, csrc_ref, ctgt_ref, coef_ref, far_ref, coarse_ref, transfer_ref, basis_ref,
    near_ref, out_ref, facc, cacc
):
    leaves, rank, width = basis_ref.shape
    cases = out_ref.shape[1]
    parents = leaves // 8
    groups = leaves // PACK
    tiles = groups + parents // PACK
    position = lax.axis_index("branch")
    slot = lane_slot((cases, PACK * rank), rank)
    facc[...] = jnp.zeros_like(facc)
    cacc[...] = jnp.zeros_like(cacc)

    def couple(src_ref, block_ref, held, shift, j):
        s = src_ref[j]
        a = jnp.maximum(s, 0)
        dev = div(a, held)
        inner = a - dev * held
        tile = div(inner, PACK)
        k = jnp.where(s < 0, -1, inner - tile * PACK)
        lhs = coef_ref[dev * tiles + shift + tile]
        lhs = jnp.where(slot == k, lhs, jnp.zeros_like(lhs))
        return dot(lhs, jnp.concatenate([block_ref[j]] * PACK, axis=0))

    unroll = 16

    def far_step(i, carry):
        terms = [couple(fsrc_ref, far_ref, leaves, 0, i * unroll + u) for u in range(unroll)]
        for u in range(unroll):
            t = jnp.clip(ftgt_ref[i * unroll + u] - position * leaves, 0, leaves - 1)
            tile = div(t, PACK)
            facc[tile] += jnp.where(slot == t - tile * PACK, terms[u], 0.0)
        return carry

    def coarse_step(i, carry):
        terms = [couple(csrc_ref, coarse_ref, parents, groups, i * unroll + u) for u in range(unroll)]
        for u in range(unroll):
            t = jnp.clip(ctgt_ref[i * unroll + u] - position * parents, 0, parents - 1)
            cacc[t] += terms[u]
        return carry

    lax.fori_loop(0, csrc_ref.shape[0] // unroll, coarse_step, 0)
    lax.fori_loop(0, fsrc_ref.shape[0] // unroll, far_step, 0)
    for g in range(groups):
        part = pl.ds(PACK * g, PACK)
        coarse = cacc[g * PACK // 8][:, :rank].astype(BF16)
        down = dot_nt(coarse, transfer_ref[part].reshape(PACK * rank, rank))
        local = (facc[g] + down).astype(BF16)
        spread = jnp.concatenate(
            [jnp.where(slot == k, local, jnp.zeros_like(local)) for k in range(PACK)], axis=0
        )
        result = dot(spread, basis_ref[part].reshape(PACK * rank, width))
        out_ref[part] = (result.reshape(PACK, cases, width) + near_ref[part]).astype(BF16)


def shards(
    loads, basis, transfer, near_blocks, near_src, near_tgt, far_blocks, far_src, far_tgt,
    coarse_blocks, coarse_src, coarse_tgt
):
    leaves, cases, width = loads.shape
    rank = basis.shape[1]
    parents = leaves // 8
    tiles = (leaves + parents) // PACK
    count = lax.axis_size("branch")
    limit = 56 * 1024 * 1024
    far4 = jnp.tile(far_blocks, (1, 1, PACK))
    coarse4 = jnp.tile(coarse_blocks, (1, 1, PACK))
    mine = pl.pallas_call(
        upward,
        out_shape=jax.ShapeDtypeStruct((tiles, cases, PACK * rank), BF16),
        in_specs=[VMEM] * 3,
        out_specs=VMEM,
        compiler_params=pltpu.CompilerParams(vmem_limit_bytes=limit),
        name="upward",
    )(loads, basis, transfer)
    coef = lax.all_gather(mine, "branch", axis=0, tiled=True)
    left = lax.ppermute(loads, "branch", [(i, i + 1) for i in range(count - 1)])
    right = lax.ppermute(loads, "branch", [(i + 1, i) for i in range(count - 1)])
    chunk = 16
    entries = near_blocks.shape[0]
    near_field = pl.pallas_call(
        near,
        grid=(entries // chunk,),
        out_shape=jax.ShapeDtypeStruct((leaves, cases, width), F32),
        in_specs=[SMEM, SMEM]
        + [pl.BlockSpec((leaves, cases, width), lambda i: (0, 0, 0))] * 3
        + [pl.BlockSpec((chunk, width, width), lambda i: (i, 0, 0))],
        out_specs=pl.BlockSpec((leaves, cases, width), lambda i: (0, 0, 0)),
        scratch_shapes=[pltpu.VMEM((3 * leaves + 1, cases, width), BF16)],
        compiler_params=pltpu.CompilerParams(vmem_limit_bytes=limit),
        cost_estimate=pl.CostEstimate(
            flops=2 * entries * cases * width * width, bytes_accessed=12 * 2**20, transcendentals=0
        ),
        name="near",
    )(near_src, near_tgt, left, loads, right, near_blocks)
    return pl.pallas_call(
        downward,
        out_shape=jax.ShapeDtypeStruct((leaves, cases, width), BF16),
        in_specs=[SMEM] * 4 + [VMEM] * 6,
        out_specs=VMEM,
        scratch_shapes=[
            pltpu.VMEM((leaves // PACK, cases, PACK * rank), F32),
            pltpu.VMEM((parents, cases, PACK * rank), F32),
        ],
        compiler_params=pltpu.CompilerParams(vmem_limit_bytes=limit),
        name="downward",
    )(far_src, far_tgt, coarse_src, coarse_tgt, coef, far4, coarse4, transfer, basis, near_field)


def solution(mesh):
    spread = P(("rve", "branch"))
    return jax.shard_map(
        shards, mesh=mesh, in_specs=(spread,) * 12, out_specs=spread, check_vma=False
    )
```

```python
import functools

import jax
import jax.numpy as jnp
from jax import lax
from jax.experimental import pallas as pl
from jax.experimental.pallas import tpu as pltpu
from jax.sharding import PartitionSpec as P

F32, BF16 = jnp.float32, jnp.bfloat16
VMEM = pl.BlockSpec(memory_space=pltpu.VMEM)
ANY = pl.BlockSpec(memory_space=pl.ANY)
SMEM = pl.BlockSpec(memory_space=pltpu.SMEM)
PACK = 4
NT = (((1,), (1,)), ((), ()))


def div(x, n):
    return lax.shift_right_logical(x, n.bit_length() - 1) if n & (n - 1) == 0 else lax.div(x, n)


def dot(a, b):
    return jnp.dot(a, b, preferred_element_type=F32)


def dot_nt(a, b):
    return lax.dot_general(a, b, NT, preferred_element_type=F32)


def lane_slot(shape, rank):
    return div(lax.broadcasted_iota(jnp.int32, shape, 1), rank)


def upward(loads_ref, basis_ref, transfer_ref, out_ref):
    leaves, cases, width = loads_ref.shape
    rank = basis_ref.shape[1]
    groups = leaves // PACK
    slot = lane_slot((cases, PACK * rank), rank)
    per_parent = 8 // PACK
    parents = []
    total = None
    for g in range(groups):
        part = pl.ds(PACK * g, PACK)
        full = dot_nt(
            loads_ref[part].reshape(PACK * cases, width), basis_ref[part].reshape(PACK * rank, width)
        )
        packed = full[:cases]
        for k in range(1, PACK):
            packed = jnp.where(slot == k, full[k * cases : (k + 1) * cases], packed)
        packed = packed.astype(BF16)
        out_ref[g] = packed
        term = dot(packed, transfer_ref[part].reshape(PACK * rank, rank))
        total = term if g % per_parent == 0 else total + term
        if g % per_parent == per_parent - 1:
            parents.append(total)
    for h in range(len(parents) // PACK):
        out_ref[groups + h] = jnp.concatenate(parents[PACK * h : PACK * h + PACK], axis=1).astype(BF16)


def exchange(
    n, loads_ref, basis_ref, transfer_ref, coef, mine, ring_send, ring_recv, pair_send, pair_recv, own_sem
):
    me = lax.axis_index("branch")
    chips = n // 2
    half = chips // 2
    core = lax.rem(me, 2)
    chip = lax.div(me, 2)
    odd = lax.rem(chip, 2)
    low = lax.div(chip, 2)
    place = low + odd * (chips - 1 - 2 * low)

    def at(position, core):
        position = lax.rem(position + chips, chips)
        far_side = lax.div(position, half)
        return 2 * (2 * position + far_side * (2 * chips - 4 * position - 1)) + core

    after, before = at(place + 1, core), at(place - 1, core)
    partner = me + 1 - 2 * core
    barrier = pltpu.get_barrier_semaphore()
    for other in (after, before, partner):
        pl.semaphore_signal(barrier, inc=1, device_id={"branch": other})
    pl.semaphore_wait(barrier, 3)

    upward(loads_ref, basis_ref, transfer_ref, mine)
    own = pltpu.make_async_copy(mine, coef.at[me], own_sem)
    own.start()

    share = mine.shape[0] // 2
    parts = [pl.ds(0, share), pl.ds(share, mine.shape[0] - share)]

    def ring(way, h, step):
        position = place - step if way == 0 else place + step
        block = coef.at[at(position, core), parts[h]]
        return pltpu.make_async_remote_copy(
            src_ref=mine.at[parts[h]] if step == 0 else block, dst_ref=block,
            send_sem=ring_send.at[way, h, step], recv_sem=ring_recv.at[way, h, step],
            device_id={"branch": after if way == 0 else before},
        )

    def pair(k, src, dst):
        return pltpu.make_async_remote_copy(
            src_ref=src, dst_ref=dst, send_sem=pair_send.at[k], recv_sem=pair_recv.at[k],
            device_id={"branch": partner},
        )

    copies = {
        (way, h, step): ring(way, h, step)
        for step in range(half)
        for h in range(2)
        for way in range(2)
        if step < half - (way != h)
    }
    for key, copy in copies.items():
        if key[2] == 0:
            copy.start()
    paired = [pair(0, mine, coef.at[me])]
    paired[0].start()
    for (way, h, step), copy in copies.items():
        copy.wait_recv()
        if (way, h, step + 1) in copies:
            copies[way, h, step + 1].start()
        position = place - 1 - step if way == 0 else place + 1 + step
        block = coef.at[at(position, core), parts[h]]
        paired.append(pair(1 + (2 * step + way) * 2 + h, block, block))
        paired[-1].start()
    for copy in paired:
        copy.wait()
    for copy in copies.values():
        copy.wait_send()
    own.wait()


def near(src_ref, tgt_ref, left_ref, own_ref, right_ref, far_ref, blocks_ref, out_ref, wide, total):
    step = pl.program_id(0)
    leaves = own_ref.shape[0]
    base = lax.axis_index("branch") * leaves
    chunk = blocks_ref.shape[0]

    @pl.when(step == 0)
    def _():
        wide[pl.ds(0, leaves)] = left_ref[...]
        wide[pl.ds(leaves, leaves)] = own_ref[...]
        wide[pl.ds(2 * leaves, leaves)] = right_ref[...]
        wide[3 * leaves] = jnp.zeros(wide.shape[1:], BF16)
        total[...] = far_ref[...]

    terms = []
    for i in range(chunk):
        s = src_ref[step * chunk + i]
        row = jnp.where(s < 0, 3 * leaves, jnp.clip(s - base + leaves, 0, 3 * leaves - 1))
        terms.append(dot(wide[row], blocks_ref[i]))
    for i in range(chunk):
        t = jnp.clip(tgt_ref[step * chunk + i] - base, 0, leaves - 1)
        total[t] += terms[i]

    @pl.when(step == pl.num_programs(0) - 1)
    def _():
        out_ref[...] = total[...].astype(BF16)


def downward(
    fsrc_ref, ftgt_ref, csrc_ref, ctgt_ref, coef_ref, far_ref, coarse_ref, transfer_ref, basis_ref,
    out_ref, facc, cacc
):
    leaves, rank, width = basis_ref.shape
    cases = out_ref.shape[1]
    parents = leaves // 8
    groups = leaves // PACK
    tiles = groups + parents // PACK
    position = lax.axis_index("branch")
    slot = lane_slot((cases, PACK * rank), rank)
    facc[...] = jnp.zeros_like(facc)
    cacc[...] = jnp.zeros_like(cacc)

    def couple(src_ref, block_ref, held, shift, j):
        s = src_ref[j]
        a = jnp.maximum(s, 0)
        dev = div(a, held)
        inner = a - dev * held
        tile = div(inner, PACK)
        k = jnp.where(s < 0, -1, inner - tile * PACK)
        lhs = coef_ref[dev * tiles + shift + tile]
        lhs = jnp.where(slot == k, lhs, jnp.zeros_like(lhs))
        return dot(lhs, jnp.concatenate([block_ref[j]] * PACK, axis=0))

    unroll = 16

    def far_step(i, carry):
        terms = [couple(fsrc_ref, far_ref, leaves, 0, i * unroll + u) for u in range(unroll)]
        for u in range(unroll):
            t = jnp.clip(ftgt_ref[i * unroll + u] - position * leaves, 0, leaves - 1)
            tile = div(t, PACK)
            facc[tile] += jnp.where(slot == t - tile * PACK, terms[u], 0.0)
        return carry

    def coarse_step(i, carry):
        terms = [couple(csrc_ref, coarse_ref, parents, groups, i * unroll + u) for u in range(unroll)]
        for u in range(unroll):
            t = jnp.clip(ctgt_ref[i * unroll + u] - position * parents, 0, parents - 1)
            cacc[t] += terms[u]
        return carry

    lax.fori_loop(0, csrc_ref.shape[0] // unroll, coarse_step, 0)
    lax.fori_loop(0, fsrc_ref.shape[0] // unroll, far_step, 0)
    for g in range(groups):
        part = pl.ds(PACK * g, PACK)
        coarse = cacc[g * PACK // 8][:, :rank].astype(BF16)
        down = dot_nt(coarse, transfer_ref[part].reshape(PACK * rank, rank))
        local = (facc[g] + down).astype(BF16)
        spread = jnp.concatenate(
            [jnp.where(slot == k, local, jnp.zeros_like(local)) for k in range(PACK)], axis=0
        )
        result = dot(spread, basis_ref[part].reshape(PACK * rank, width))
        out_ref[part] = result.reshape(PACK, cases, width)


def shards(
    loads, basis, transfer, near_blocks, near_src, near_tgt, far_blocks, far_src, far_tgt,
    coarse_blocks, coarse_src, coarse_tgt
):
    leaves, cases, width = loads.shape
    rank = basis.shape[1]
    parents = leaves // 8
    tiles = (leaves + parents) // PACK
    count = lax.axis_size("branch")
    limit = 56 * 1024 * 1024
    far4 = jnp.tile(far_blocks, (1, 1, PACK))
    coarse4 = jnp.tile(coarse_blocks, (1, 1, PACK))
    half = count // 4
    left = lax.ppermute(loads, "branch", [(i, i + 1) for i in range(count - 1)])
    right = lax.ppermute(loads, "branch", [(i + 1, i) for i in range(count - 1)])
    (coef,) = pl.pallas_call(
        functools.partial(exchange, count),
        out_shape=(
            jax.ShapeDtypeStruct((count, tiles, cases, PACK * rank), BF16),
        ),
        in_specs=[VMEM] * 3,
        out_specs=(ANY,),
        scratch_shapes=[
            pltpu.VMEM((tiles, cases, PACK * rank), BF16),
            pltpu.SemaphoreType.DMA((2, 2, half)),
            pltpu.SemaphoreType.DMA((2, 2, half)),
            pltpu.SemaphoreType.DMA((1 + 4 * half,)),
            pltpu.SemaphoreType.DMA((1 + 4 * half,)),
            pltpu.SemaphoreType.DMA,
        ],
        compiler_params=pltpu.CompilerParams(
            collective_id=0, has_side_effects=True, vmem_limit_bytes=limit
        ),
        name="exchange",
    )(loads, basis, transfer)
    coef = coef.reshape(count * tiles, cases, PACK * rank)
    chunk = 16
    entries = near_blocks.shape[0]
    far_field = pl.pallas_call(
        downward,
        out_shape=jax.ShapeDtypeStruct((leaves, cases, width), F32),
        in_specs=[SMEM] * 4 + [VMEM] * 5,
        out_specs=VMEM,
        scratch_shapes=[
            pltpu.VMEM((leaves // PACK, cases, PACK * rank), F32),
            pltpu.VMEM((parents, cases, PACK * rank), F32),
        ],
        compiler_params=pltpu.CompilerParams(vmem_limit_bytes=limit),
        name="downward",
    )(far_src, far_tgt, coarse_src, coarse_tgt, coef, far4, coarse4, transfer, basis)
    return pl.pallas_call(
        near,
        grid=(entries // chunk,),
        out_shape=jax.ShapeDtypeStruct((leaves, cases, width), BF16),
        in_specs=[SMEM, SMEM]
        + [pl.BlockSpec((leaves, cases, width), lambda i: (0, 0, 0))] * 4
        + [pl.BlockSpec((chunk, width, width), lambda i: (i, 0, 0))],
        out_specs=pl.BlockSpec((leaves, cases, width), lambda i: (0, 0, 0)),
        scratch_shapes=[
            pltpu.VMEM((3 * leaves + 1, cases, width), BF16),
            pltpu.VMEM((leaves, cases, width), F32),
        ],
        compiler_params=pltpu.CompilerParams(vmem_limit_bytes=limit),
        cost_estimate=pl.CostEstimate(
            flops=2 * entries * cases * width * width, bytes_accessed=12 * 2**20, transcendentals=0
        ),
        name="near",
    )(near_src, near_tgt, left, loads, right, far_field, near_blocks)


def solution(mesh):
    spread = P(("rve", "branch"))
    return jax.shard_map(
        shards, mesh=mesh, in_specs=(spread,) * 12, out_specs=spread, check_vma=False
    )
```

```python
import functools

import jax
import jax.numpy as jnp
from jax import lax
from jax.experimental import pallas as pl
from jax.experimental.pallas import tpu as pltpu
from jax.sharding import PartitionSpec as P

F32, BF16 = jnp.float32, jnp.bfloat16
VMEM = pl.BlockSpec(memory_space=pltpu.VMEM)
ANY = pl.BlockSpec(memory_space=pl.ANY)
SMEM = pl.BlockSpec(memory_space=pltpu.SMEM)
PACK = 4
NT = (((1,), (1,)), ((), ()))


def div(x, n):
    return lax.shift_right_logical(x, n.bit_length() - 1) if n & (n - 1) == 0 else lax.div(x, n)


def dot(a, b):
    return jnp.dot(a, b, preferred_element_type=F32)


def dot_nt(a, b):
    return lax.dot_general(a, b, NT, preferred_element_type=F32)


def lane_slot(shape, rank):
    return div(lax.broadcasted_iota(jnp.int32, shape, 1), rank)


def upward(loads_ref, basis_ref, transfer_ref, out_ref):
    leaves, cases, width = loads_ref.shape
    rank = basis_ref.shape[1]
    groups = leaves // PACK
    slot = lane_slot((cases, PACK * rank), rank)
    per_parent = 8 // PACK
    parents = []
    total = None
    for g in range(groups):
        part = pl.ds(PACK * g, PACK)
        full = dot_nt(
            loads_ref[part].reshape(PACK * cases, width), basis_ref[part].reshape(PACK * rank, width)
        )
        packed = full[:cases]
        for k in range(1, PACK):
            packed = jnp.where(slot == k, full[k * cases : (k + 1) * cases], packed)
        packed = packed.astype(BF16)
        out_ref[g] = packed
        term = dot(packed, transfer_ref[part].reshape(PACK * rank, rank))
        total = term if g % per_parent == 0 else total + term
        if g % per_parent == per_parent - 1:
            parents.append(total)
    for h in range(len(parents) // PACK):
        out_ref[groups + h] = jnp.concatenate(parents[PACK * h : PACK * h + PACK], axis=1).astype(BF16)


def exchange(
    n, loads_ref, basis_ref, transfer_ref, coef, mine, ring_send, ring_recv, pair_send, pair_recv, own_sem
):
    me = lax.axis_index("branch")
    chips = n // 2
    half = chips // 2
    core = lax.rem(me, 2)
    chip = lax.div(me, 2)
    odd = lax.rem(chip, 2)
    low = lax.div(chip, 2)
    place = low + odd * (chips - 1 - 2 * low)

    def at(position, core):
        position = lax.rem(position + chips, chips)
        far_side = lax.div(position, half)
        return 2 * (2 * position + far_side * (2 * chips - 4 * position - 1)) + core

    after, before = at(place + 1, core), at(place - 1, core)
    partner = me + 1 - 2 * core
    barrier = pltpu.get_barrier_semaphore()
    for other in (after, before, partner):
        pl.semaphore_signal(barrier, inc=1, device_id={"branch": other})
    pl.semaphore_wait(barrier, 3)

    upward(loads_ref, basis_ref, transfer_ref, mine)
    own = pltpu.make_async_copy(mine, coef.at[me], own_sem)
    own.start()

    share = mine.shape[0] // 2
    parts = [pl.ds(0, share), pl.ds(share, mine.shape[0] - share)]

    def ring(way, h, step):
        position = place - step if way == 0 else place + step
        block = coef.at[at(position, core), parts[h]]
        return pltpu.make_async_remote_copy(
            src_ref=mine.at[parts[h]] if step == 0 else block, dst_ref=block,
            send_sem=ring_send.at[way, h, step], recv_sem=ring_recv.at[way, h, step],
            device_id={"branch": after if way == 0 else before},
        )

    def pair(k, src, dst):
        return pltpu.make_async_remote_copy(
            src_ref=src, dst_ref=dst, send_sem=pair_send.at[k], recv_sem=pair_recv.at[k],
            device_id={"branch": partner},
        )

    copies = {
        (way, h, step): ring(way, h, step)
        for step in range(half)
        for h in range(2)
        for way in range(2)
        if step < half - (way != h)
    }
    for key, copy in copies.items():
        if key[2] == 0:
            copy.start()
    paired = [pair(0, mine, coef.at[me])]
    paired[0].start()
    for (way, h, step), copy in copies.items():
        copy.wait_recv()
        if (way, h, step + 1) in copies:
            copies[way, h, step + 1].start()
        position = place - 1 - step if way == 0 else place + 1 + step
        block = coef.at[at(position, core), parts[h]]
        paired.append(pair(1 + (2 * step + way) * 2 + h, block, block))
        paired[-1].start()
    for copy in paired:
        copy.wait()
    for copy in copies.values():
        copy.wait_send()
    own.wait()


def near(src_ref, tgt_ref, left_ref, own_ref, right_ref, far_ref, blocks_ref, out_ref, wide, total):
    step = pl.program_id(0)
    leaves = own_ref.shape[0]
    base = lax.axis_index("branch") * leaves
    chunk = blocks_ref.shape[0]

    @pl.when(step == 0)
    def _():
        wide[pl.ds(0, leaves)] = left_ref[...]
        wide[pl.ds(leaves, leaves)] = own_ref[...]
        wide[pl.ds(2 * leaves, leaves)] = right_ref[...]
        wide[3 * leaves] = jnp.zeros(wide.shape[1:], BF16)
        total[...] = far_ref[...]

    for first in range(0, chunk, 16):
        terms = []
        for i in range(first, first + 16):
            s = src_ref[step * chunk + i]
            row = jnp.where(s < 0, 3 * leaves, jnp.clip(s - base + leaves, 0, 3 * leaves - 1))
            terms.append(dot(wide[row], blocks_ref[i]))
        for i in range(first, first + 16):
            t = jnp.clip(tgt_ref[step * chunk + i] - base, 0, leaves - 1)
            total[t] += terms[i - first]

    @pl.when(step == pl.num_programs(0) - 1)
    def _():
        out_ref[...] = total[...].astype(BF16)


def downward(
    fsrc_ref, ftgt_ref, csrc_ref, ctgt_ref, coef_ref, far_ref, coarse_ref, transfer_ref, basis_ref,
    out_ref, facc, cacc
):
    leaves, rank, width = basis_ref.shape
    cases = out_ref.shape[1]
    parents = leaves // 8
    groups = leaves // PACK
    tiles = groups + parents // PACK
    position = lax.axis_index("branch")
    slot = lane_slot((cases, PACK * rank), rank)
    facc[...] = jnp.zeros_like(facc)
    cacc[...] = jnp.zeros_like(cacc)

    def couple(src_ref, block_ref, held, shift, j):
        s = src_ref[j]
        a = jnp.maximum(s, 0)
        dev = div(a, held)
        inner = a - dev * held
        tile = div(inner, PACK)
        k = jnp.where(s < 0, -1, inner - tile * PACK)
        lhs = coef_ref[dev * tiles + shift + tile]
        lhs = jnp.where(slot == k, lhs, jnp.zeros_like(lhs))
        return dot(lhs, jnp.concatenate([block_ref[j]] * PACK, axis=0))

    unroll = 64

    def far_step(i, carry):
        terms = [couple(fsrc_ref, far_ref, leaves, 0, i * unroll + u) for u in range(unroll)]
        for u in range(unroll):
            t = jnp.clip(ftgt_ref[i * unroll + u] - position * leaves, 0, leaves - 1)
            tile = div(t, PACK)
            facc[tile] += jnp.where(slot == t - tile * PACK, terms[u], 0.0)
        return carry

    def coarse_step(i, carry):
        terms = [couple(csrc_ref, coarse_ref, parents, groups, i * unroll + u) for u in range(unroll)]
        for u in range(unroll):
            t = jnp.clip(ctgt_ref[i * unroll + u] - position * parents, 0, parents - 1)
            cacc[t] += terms[u]
        return carry

    lax.fori_loop(0, csrc_ref.shape[0] // unroll, coarse_step, 0)
    lax.fori_loop(0, fsrc_ref.shape[0] // unroll, far_step, 0)
    for g in range(groups):
        part = pl.ds(PACK * g, PACK)
        coarse = cacc[g * PACK // 8][:, :rank].astype(BF16)
        down = dot_nt(coarse, transfer_ref[part].reshape(PACK * rank, rank))
        local = (facc[g] + down).astype(BF16)
        spread = jnp.concatenate(
            [jnp.where(slot == k, local, jnp.zeros_like(local)) for k in range(PACK)], axis=0
        )
        result = dot(spread, basis_ref[part].reshape(PACK * rank, width))
        out_ref[part] = result.reshape(PACK, cases, width)


def shards(
    loads, basis, transfer, near_blocks, near_src, near_tgt, far_blocks, far_src, far_tgt,
    coarse_blocks, coarse_src, coarse_tgt
):
    leaves, cases, width = loads.shape
    rank = basis.shape[1]
    parents = leaves // 8
    tiles = (leaves + parents) // PACK
    count = lax.axis_size("branch")
    limit = 56 * 1024 * 1024
    far4 = jnp.tile(far_blocks, (1, 1, PACK))
    coarse4 = jnp.tile(coarse_blocks, (1, 1, PACK))
    half = count // 4
    left = lax.ppermute(loads, "branch", [(i, i + 1) for i in range(count - 1)])
    right = lax.ppermute(loads, "branch", [(i + 1, i) for i in range(count - 1)])
    (coef,) = pl.pallas_call(
        functools.partial(exchange, count),
        out_shape=(
            jax.ShapeDtypeStruct((count, tiles, cases, PACK * rank), BF16),
        ),
        in_specs=[VMEM] * 3,
        out_specs=(ANY,),
        scratch_shapes=[
            pltpu.VMEM((tiles, cases, PACK * rank), BF16),
            pltpu.SemaphoreType.DMA((2, 2, half)),
            pltpu.SemaphoreType.DMA((2, 2, half)),
            pltpu.SemaphoreType.DMA((1 + 4 * half,)),
            pltpu.SemaphoreType.DMA((1 + 4 * half,)),
            pltpu.SemaphoreType.DMA,
        ],
        compiler_params=pltpu.CompilerParams(
            collective_id=0, has_side_effects=True, vmem_limit_bytes=limit
        ),
        name="exchange",
    )(loads, basis, transfer)
    coef = coef.reshape(count * tiles, cases, PACK * rank)
    chunk = 32
    entries = near_blocks.shape[0]
    far_field = pl.pallas_call(
        downward,
        out_shape=jax.ShapeDtypeStruct((leaves, cases, width), F32),
        in_specs=[SMEM] * 4 + [VMEM] * 5,
        out_specs=VMEM,
        scratch_shapes=[
            pltpu.VMEM((leaves // PACK, cases, PACK * rank), F32),
            pltpu.VMEM((parents, cases, PACK * rank), F32),
        ],
        compiler_params=pltpu.CompilerParams(vmem_limit_bytes=limit),
        name="downward",
    )(far_src, far_tgt, coarse_src, coarse_tgt, coef, far4, coarse4, transfer, basis)
    return pl.pallas_call(
        near,
        grid=(entries // chunk,),
        out_shape=jax.ShapeDtypeStruct((leaves, cases, width), BF16),
        in_specs=[SMEM, SMEM]
        + [pl.BlockSpec((leaves, cases, width), lambda i: (0, 0, 0))] * 4
        + [pl.BlockSpec((chunk, width, width), lambda i: (i, 0, 0))],
        out_specs=pl.BlockSpec((leaves, cases, width), lambda i: (0, 0, 0)),
        scratch_shapes=[
            pltpu.VMEM((3 * leaves + 1, cases, width), BF16),
            pltpu.VMEM((leaves, cases, width), F32),
        ],
        compiler_params=pltpu.CompilerParams(vmem_limit_bytes=limit),
        cost_estimate=pl.CostEstimate(
            flops=2 * entries * cases * width * width, bytes_accessed=12 * 2**20, transcendentals=0
        ),
        name="near",
    )(near_src, near_tgt, left, loads, right, far_field, near_blocks)


def solution(mesh):
    spread = P(("rve", "branch"))
    return jax.shard_map(
        shards, mesh=mesh, in_specs=(spread,) * 12, out_specs=spread, check_vma=False
    )
```
